512 devices in a mesh: prow: 16 (over y, x_lo), pcol: 32 (over x_hi, z, core).
Axes of the slice: x: 4 (x_hi: 2, x_lo: 2; x = x_hi * 2 + x_lo), y: 8, z: 8, core: 2. Of those that a mesh axis runs over, the one named last changes fastest.
Arguments:
- matrix: float32 [12288, 12288], P('prow', 'pcol'), may hold values from -6 to 6, as said below
- reflectors: float32 [12288, 512], P('prow'), may hold values from -0.0546875 to 0.0546875
- factors: float32 [2, 256, 256], replicated, may hold values from -0.25 to 2, as said below
Outputs:
- updated: float32 [12288, 12288], P('prow', 'pcol')
The draws below stay inside these ranges and needn't reach their ends.
Inputs may be any that keep to these rules, and one draw needn't show every extreme that they name: `matrix`: symmetric: entry (i, j) equals entry (j, i). `factors`: each of the 2 blocks is upper triangular with diagonal entries between 1 and 2.
All inputs are finite; a program needn't handle non-finite values.
Results may differ from the reference program's by a relative error of at most 0.0001.
Values sent between devices are 32-bit elements; how exact they have to be, the bound alone decides.
A program may use at most 64 MiB of HBM per device.

```python
import jax
import jax.numpy as jnp
from jax import lax

N = 12288
NB = 256
PANELS = 2


def draw_matrix(key, part):
    value_key = jax.random.fold_in(key, 11)
    values = jnp.clip(jax.random.normal(value_key, (N, N), jnp.float32), -4.0, 4.0)
    return (values + values.T) * 0.7071


def draw_factors(key, part):
    diag_key = jax.random.fold_in(key, 21)
    upper_key = jax.random.fold_in(key, 22)
    upper = jnp.clip(0.05 * jax.random.normal(upper_key, (PANELS, NB, NB), jnp.float32), -0.25, 0.25)
    diagonal = jax.random.uniform(diag_key, (PANELS, NB), jnp.float32, 1.0, 2.0)
    row_ids = lax_iota_rows()
    above = (row_ids[1][None, :, :] > row_ids[0][None, :, :]).astype(jnp.float32)
    same = (row_ids[1][None, :, :] == row_ids[0][None, :, :]).astype(jnp.float32)
    return upper * above + same * diagonal[:, :, None]


def lax_iota_rows():
    rows_ids = jnp.arange(NB)[:, None] * jnp.ones((1, NB), jnp.int32)
    cols_ids = jnp.arange(NB)[None, :] * jnp.ones((NB, 1), jnp.int32)
    return (rows_ids, cols_ids)


def levels(stream_key, shape, shards, least, largest):
    level = 1.0
    for position, shards_of in shards:
        steps = jax.random.uniform(jax.random.fold_in(jax.random.fold_in(stream_key, 6), position), (shards_of,), jnp.float32, least / len(shards), largest / len(shards))
        level = level * jnp.repeat(jnp.exp(steps), shape[position] // shards_of).reshape((-1,) + (1,) * (len(shape) - 1 - position))
    return level


def gaussian(rng, extent, deviation, limit, split=(), kind=jnp.bfloat16):
    factor_of = levels(rng, extent, split, -0.22, 0.18) if split else 1.0
    drawn = jax.random.normal(rng, extent, jnp.float32) * deviation * factor_of
    return jnp.minimum(jnp.maximum(drawn, -limit), limit).astype(kind)


def setup_inputs(seed: int = 0) -> dict:
    splits = jax.random.split(jax.random.key(seed), 4)
    return {
        "matrix": draw_matrix(jax.random.fold_in(splits[3], 71), 0),
        "reflectors": gaussian(splits[1], (N, PANELS * NB), N ** -0.5, 0.0546875, ((0, 16),), jnp.float32),
        "factors": draw_factors(jax.random.fold_in(splits[3], 71), 0),
    }


def high_dot(left, right):
    return jnp.dot(left, right, precision=lax.Precision.HIGHEST, preferred_element_type=jnp.float32)


def inner_dot(left, right):
    return lax.dot_general(left, right, (((0,), (0,)), ((), ())), precision=lax.Precision.HIGHEST, preferred_element_type=jnp.float32)


def outer_dot(left, right):
    return lax.dot_general(left, right, (((1,), (1,)), ((), ())), precision=lax.Precision.HIGHEST, preferred_element_type=jnp.float32)


def reference(matrix, reflectors, factors):
    current = matrix
    for panel in range(PANELS):
        vectors = reflectors[:, panel * NB:(panel + 1) * NB]
        factor = factors[panel]
        projected = high_dot(high_dot(current, vectors), factor)
        coupling = inner_dot(factor, inner_dot(vectors, projected))
        corrected = projected - 0.5 * high_dot(vectors, coupling)
        current = current - outer_dot(vectors, corrected) - outer_dot(corrected, vectors)
    return current
```

```python
import jax
import jax.numpy as jnp
from jax import lax
from jax.experimental import pallas as pl
from jax.experimental.pallas import tpu as pltpu
from jax.sharding import PartitionSpec as P

F32 = jnp.float32
BF16 = jnp.bfloat16
RING = 8
NN = (((1,), (0,)), ((), ()))
TN = (((0,), (0,)), ((), ()))
NT = (((1,), (1,)), ((), ()))


def split(x):
    high = x.astype(BF16)
    return high, (x - high.astype(F32)).astype(BF16)


def dot3(left, right, dims):
    (lh, ll), (rh, rl) = left, right
    def one(p, q):
        return lax.dot_general(p, q, dims, preferred_element_type=F32)
    return one(lh, rh) + (one(lh, rl) + one(ll, rh))


def mm(left, right, dims):
    return dot3(split(left), split(right), dims)


def kernel(a_ref, v_ref, t_ref, upd_ref, vh, vl, pt, rs_recv, zx_recv, zcol, vcol, zrow, s21, gloc,
           ga_recv, gb_recv, gtiles, gc_recv, gfull, qh, ql, uh, ul, yt1_ref, send_sems, recv_sems):
    rows, width = v_ref.shape
    cols = a_ref.shape[1]
    nb = width // 2
    sub = width // 16
    vsub = cols // 16
    r = lax.axis_index("prow")
    c = lax.axis_index("pcol")
    y, xl = r // 2, r % 2
    chip, k = c // 2, c % 2
    xh, z = chip // 8, chip % 8

    y_up, y_down = ((y + 1) % RING * 2 + xl, c), ((y + RING - 1) % RING * 2 + xl, c)
    z_up = (r, (xh * 8 + (z + 1) % RING) * 2 + k)
    z_down = (r, (xh * 8 + (z + RING - 1) % RING) * 2 + k)
    x_near = (y * 2 + 1 - xl, c)
    x_far = (r, ((1 - xh) * 8 + z) * 2 + k)
    other = (r, chip * 2 + 1 - k)
    mirror = (chip, r * 2 + k)
    apart = r != chip

    count = [0]
    started = []

    def copy(src, dst, device):
        slot = count[0]
        count[0] += 1
        return pltpu.make_async_remote_copy(
            src_ref=src, dst_ref=dst, send_sem=send_sems.at[slot], recv_sem=recv_sems.at[slot],
            device_id=device, device_id_type=pl.DeviceIdType.MESH)

    def go(op):
        op.start()
        started.append(op)
        return op

    barrier = pltpu.get_barrier_semaphore()
    y_peers = [((y + o) % RING * 2 + xl, c) for o in range(1, RING)]
    fixed = [*y_peers, x_near, z_up, z_down, x_far, other]
    for device in fixed:
        pl.semaphore_signal(barrier, inc=1, device_id=device, device_id_type=pl.DeviceIdType.MESH)

    @pl.when(apart)
    def _():
        pl.semaphore_signal(barrier, inc=1, device_id=mirror, device_id_type=pl.DeviceIdType.MESH)

    high, low = split(v_ref[...])
    vh[...] = high
    vl[...] = low
    a_split = split(a_ref[...])
    for j in range(width // 128):
        lanes = slice(j * 128, (j + 1) * 128)
        pt[lanes, :] = dot3((vh[:, lanes], vl[:, lanes]), a_split, TN)

    pl.semaphore_wait(barrier, len(fixed) + apart.astype(jnp.int32))

    v_out = v_ref.at[pl.ds(pl.multiple_of(k * cols + chip // 2 * 2 * vsub, 8), 2 * vsub), :]
    v_to = vcol.at[pl.ds(pl.multiple_of(chip // 2 * 2 * vsub, 8), 2 * vsub), :]
    v_copy = copy(v_out, v_to, mirror)

    def pt_at(half, index):
        return pl.ds(pl.multiple_of((index + RING) % RING * (2 * sub) + half * sub, sub), sub)

    def rs_op(name, s):
        right = name[0] == "R"
        half = 0 if name[1] == "A" else 1
        index = y + 4 - s if right else y - 4 + s
        slot = {"RA": 0, "LB": 4, "RB": 8 - 1, "LA": 11 - 1}[name] + s
        return copy(pt.at[pt_at(half, index), :], rs_recv.at[slot], y_up if right else y_down), slot

    first = {"RA": 0, "LB": 0, "RB": 1, "LA": 1}
    rs = {}
    for name in ("RA", "LB", "RB", "LA"):
        rs[name, first[name]] = rs_op(name, first[name])
        go(rs[name, first[name]][0])

    @pl.when(apart)
    def _():
        v_copy.start()

    @pl.when(jnp.logical_not(apart))
    def _():
        vcol[pl.ds(pl.multiple_of(chip // 2 * 2 * vsub, 8), 2 * vsub), :] = (
            v_ref[pl.ds(pl.multiple_of(k * cols + chip // 2 * 2 * vsub, 8), 2 * vsub), :])

    half_rows = pl.ds(pl.multiple_of(k * cols, 128), cols)
    s21[...] = dot3((vh[half_rows, nb:], vl[half_rows, nb:]), (vh[half_rows, :nb], vl[half_rows, :nb]), TN)

    for s in range(1, 4):
        for name in ("RA", "LB", "RB", "LA"):
            if s - 1 < first[name]:
                continue
            op, slot = rs[name, s - 1]
            op.wait_recv()
            half = 0 if name[1] == "A" else 1
            index = y + 4 - s if name[0] == "R" else y - 4 + s
            at = pt_at(half, index)
            pt[at, :] = pt[at, :] + rs_recv[slot]
            rs[name, s] = rs_op(name, s)
            go(rs[name, s][0])
    for half, names in ((0, ("RA", "LA")), (1, ("LB", "RB"))):
        at = pt_at(half, y)
        total = pt[at, :]
        for name in names:
            op, slot = rs[name, 3]
            op.wait_recv()
            total = total + rs_recv[slot]
        pt[at, :] = total

    x_ops = []
    for which in range(2):
        half = (1 - xl) if which == 0 else xl
        x_ops.append(go(copy(pt.at[pt_at(half, y), :], zx_recv.at[pl.ds(pl.multiple_of(half * sub, sub), sub), :], x_near)))

    @pl.when(apart)
    def _():
        v_copy.wait_recv()

    def ring(ref_of, me, up, down):
        ops = {}
        def start(name, s):
            right = name[0] == "R"
            index = (me - s + RING) % RING if right else (me + s) % RING
            ref = ref_of(0 if name[1] == "A" else 1, index)
            ops[name, s] = go(copy(ref, ref, up if right else down))
        last = {"RA": 3, "LB": 3, "RB": 2, "LA": 2}
        def step(s, arrived=None):
            for name in ("RA", "LB", "RB", "LA"):
                if s >= 1 and s - 1 <= last[name]:
                    ops[name, s - 1].wait_recv()
                if s <= last[name]:
                    start(name, s)
                if arrived is not None and s >= 1 and s - 1 <= last[name]:
                    index = (me - s + RING) % RING if name[0] == "R" else (me + s) % RING
                    arrived(0 if name[1] == "A" else 1, index)
        return step

    v_ring = ring(lambda h, i: vcol.at[pl.ds(pl.multiple_of(i * 2 * vsub + h * vsub, 8), vsub), :], y, y_up, y_down)
    z_ring = ring(lambda h, i: zcol.at[pt_at(h, i), :], y, y_up, y_down)

    def zrow_at(core, h, i):
        return zrow.at[core, pl.ds(pl.multiple_of((h * 8 + i) * sub, sub), sub), :]

    row_ring = ring(lambda h, i: zrow_at(k, h, i), z, z_up, z_down)
    g_ring = ring(lambda h, i: gfull.at[(h * 8 + i) * 2 + k], z, z_up, z_down)
    to_other = []

    def pass_row(h, i):
        to_other.append(go(copy(zrow_at(k, h, i), zrow_at(k, h, i), other)))

    def pass_g(h, i):
        ref = gfull.at[(h * 8 + i) * 2 + k]
        to_other.append(go(copy(ref, ref, other)))

    own = pt_at(xl, y)
    x_ops[0].wait_recv()
    zcol[own, :] = pt[own, :] + zx_recv[pl.ds(pl.multiple_of(xl * sub, sub), sub), :]
    row_to = zrow.at[k, pl.ds(pl.multiple_of(r * sub, sub), sub), :]
    z_copy = copy(zcol.at[own, :], row_to, mirror)

    @pl.when(apart)
    def _():
        z_copy.start()

    @pl.when(jnp.logical_not(apart))
    def _():
        zrow[k, pl.ds(pl.multiple_of(r * sub, sub), sub), :] = zcol[own, :]

    x_ops[1].wait_recv()
    rest = pt_at(1 - xl, y)
    zcol[rest, :] = pt[rest, :] + zx_recv[pl.ds(pl.multiple_of((1 - xl) * sub, sub), sub), :]
    z_ring(0)
    v_ring(0)

    @pl.when(apart)
    def _():
        z_copy.wait_recv()

    mine = zrow_at(k, xh, z)
    far_op = go(copy(mine, mine, x_far))
    slice_rows = pl.ds(pl.multiple_of(chip * sub, sub), sub)
    part = dot3(split(zrow[k, slice_rows, :]), (vh[half_rows, :], vl[half_rows, :]), NN)
    late = chip >= 8
    s_rows = s21[pl.ds(pl.multiple_of(chip % 8 * sub, sub), sub), :]
    gloc[:, :nb] = jnp.where(late, s_rows, part[:, :nb])
    gloc[:, nb:] = part[:, nb:]
    half = sub // 2
    ga = go(copy(gloc.at[pl.ds(pl.multiple_of((1 - k) * half, half), half), :], ga_recv, other))
    pass_row(xh, z)
    z_ring(1)
    ga.wait_recv()
    my_half = pl.ds(pl.multiple_of(k * half, half), half)
    gloc[my_half, :] = gloc[my_half, :] + ga_recv[...]
    gb = go(copy(gloc.at[my_half, :], gb_recv, x_near))
    far_op.wait_recv()
    row_ring(0)
    pass_row(1 - xh, z)
    v_ring(1)
    gb.wait_recv()
    total = gloc[my_half, :] + gb_recv[...]
    for j in range(8):
        gtiles[j] = total[j // 4 * 8:j // 4 * 8 + 8, j % 4 * 128:(j % 4 + 1) * 128]
    gc = [go(copy(gtiles.at[(y + o) % RING], gc_recv.at[o], y_peers[o - 1])) for o in range(1, RING)]
    row_ring(1, pass_row)
    z_ring(2)
    tile = gtiles[y]
    for o in range(1, RING):
        gc[o - 1].wait_recv()
        tile = tile + gc_recv[o]
    gfull[c, y] = tile
    gd = [go(copy(gfull.at[c, y], gfull.at[c, y], y_peers[o - 1])) for o in range(1, RING)]
    v_ring(2)
    row_ring(2, pass_row)
    for op in gd:
        op.wait_recv()
    ge = go(copy(gfull.at[c], gfull.at[c], x_far))
    pass_g(xh, z)
    z_ring(3)
    v_ring(3)
    ge.wait_recv()
    g_ring(0)
    pass_g(1 - xh, z)
    row_ring(3, pass_row)
    z_ring(4)
    g_ring(1, pass_g)
    v_ring(4)
    row_ring(4, pass_row)
    g_ring(2, pass_g)

    t1, t2 = split(t_ref[0]), split(t_ref[1])
    yt1 = dot3(t1, split(zcol[:nb, :]), TN)
    yt1_ref[...] = yt1
    qh[:nb, :], ql[:nb, :] = split(yt1)
    qh[nb:, :], ql[nb:, :] = split(dot3(t2, split(zcol[nb:, :]), TN))
    g_ring(3, pass_g)
    v1, v2 = split(vcol[:, :nb]), split(vcol[:, nb:])
    uh[:nb, :], ul[:nb, :] = split(dot3(t1, v1, NT))
    uh[nb:, :], ul[nb:, :] = split(dot3(t2, v2, NT))
    g_ring(4, pass_g)
    for op in to_other:
        op.wait_recv()

    def sweep(depth, first_pass):
        for h in range(2):
            def body(i, _, h=h):
                at = pl.ds(pl.multiple_of(h * cols + i * 128, 128), 128)
                lanes = pl.ds(pl.multiple_of(i * 128, 128), 128)
                acc = dot3((vh[at, :], vl[at, :]), (qh[...], ql[...]), NN)
                acc = acc + dot3(split(zrow[h, :depth, lanes]), (uh[:depth, :], ul[:depth, :]), TN)
                upd_ref[at, :] = -acc if first_pass else upd_ref[at, :] - acc
                return 0
            lax.fori_loop(0, cols // 128, body, 0)

    sweep(width, True)


    def block(row, col):
        parts = []
        for lane in range(2):
            j = col * 2 + lane
            both = [gfull[row * 16:(row + 1) * 16, h * 4 + j] for h in range(2)]
            parts.append(jnp.stack(both, axis=1).reshape(nb, 128))
        return jnp.concatenate(parts, axis=1)

    g11, g12, s_21, g22 = block(0, 0), block(0, 1), block(1, 0), block(1, 1)
    s_21s = split(s_21)
    s_12 = s_21.T
    s_12s = split(s_12)
    e = dot3(s_12s, t2, NN)
    es = split(e)
    m1 = dot3(t1, split(dot3(split(g11), t1, NN)), TN)
    m1s = split(m1)
    kk = dot3(t1, split(g12), TN) - 0.5 * dot3(m1s, s_12s, TN)
    kks = split(kk)
    jj = dot3(s_21s, kks, NN)
    m2 = dot3(t2, split(dot3(split(g22 - jj - jj.T), t2, NN)), TN)
    h12s = split(0.5 * dot3(m1s, es, NN) - dot3(kks, t2, NN))
    qh[:nb, :], ql[:nb, :] = split(dot3(h12s, v2, NT) - dot3(m1s, v1, NT))
    low_q = dot3(h12s, v1, (((0,), (1,)), ((), ()))) - dot3(split(m2), v2, NT)
    qh[nb:, :], ql[nb:, :] = split(low_q - dot3(es, split(yt1_ref[...]), TN))
    uh[:nb, :], ul[:nb, :] = split(-dot3(t1, split(dot3(es, v2, NT)), NN))
    sweep(nb, False)

    for op in started:
        op.wait_send()

    @pl.when(apart)
    def _():
        v_copy.wait_send()
        z_copy.wait_send()


COPIES = 14 + 2 + 2 + 14 + 14 + (1 + 14 + 16) + (1 + 1 + 7 + 7 + 1 + 14 + 16)


def body(matrix, reflectors, factors):
    rows, cols = matrix.shape
    width = reflectors.shape[1]
    nb = width // 2
    sub = width // 16
    vmem = pl.BlockSpec(memory_space=pltpu.VMEM)
    update = pl.pallas_call(
        kernel,
        out_shape=jax.ShapeDtypeStruct((rows, cols), F32),
        in_specs=[vmem] * 3,
        out_specs=vmem,
        scratch_shapes=[
            pltpu.VMEM((rows, width), BF16),
            pltpu.VMEM((rows, width), BF16),
            pltpu.VMEM((width, cols), F32),
            pltpu.VMEM((14, sub, cols), F32),
            pltpu.VMEM((2 * sub, cols), F32),
            pltpu.VMEM((width, cols), F32),
            pltpu.VMEM((cols, width), F32),
            pltpu.VMEM((2, width, cols), F32),
            pltpu.VMEM((nb, nb), F32),
            pltpu.VMEM((sub, width), F32),
            pltpu.VMEM((sub // 2, width), F32),
            pltpu.VMEM((sub // 2, width), F32),
            pltpu.VMEM((8, 8, 128), F32),
            pltpu.VMEM((8, 8, 128), F32),
            pltpu.VMEM((32, 8, 8, 128), F32),
            pltpu.VMEM((width, cols), BF16),
            pltpu.VMEM((width, cols), BF16),
            pltpu.VMEM((width, cols), BF16),
            pltpu.VMEM((width, cols), BF16),
            pltpu.VMEM((nb, cols), F32),
            pltpu.SemaphoreType.DMA((COPIES,)),
            pltpu.SemaphoreType.DMA((COPIES,)),
        ],
        compiler_params=pltpu.CompilerParams(
            collective_id=0, has_side_effects=True, vmem_limit_bytes=48 * 1024 * 1024),
        name="two_panels",
    )(matrix, reflectors, factors)
    return matrix + update


def solution(mesh):
    return jax.shard_map(
        body,
        mesh=mesh,
        in_specs=(P("prow", "pcol"), P("prow", None), P()),
        out_specs=P("prow", "pcol"),
        check_vma=False,
    )
```

```python
import jax
import jax.numpy as jnp
from jax import lax
from jax.experimental import pallas as pl
from jax.experimental.pallas import tpu as pltpu
from jax.sharding import PartitionSpec as P

F32 = jnp.float32
BF16 = jnp.bfloat16
RING = 8
NN = (((1,), (0,)), ((), ()))
TN = (((0,), (0,)), ((), ()))
NT = (((1,), (1,)), ((), ()))


def split(x):
    high = x.astype(BF16)
    return high, (x - high.astype(F32)).astype(BF16)


def dot3(left, right, dims):
    (lh, ll), (rh, rl) = left, right
    def one(p, q):
        return lax.dot_general(p, q, dims, preferred_element_type=F32)
    return one(lh, rh) + (one(lh, rl) + one(ll, rh))


def mm(left, right, dims):
    return dot3(split(left), split(right), dims)


def slot_of(q):
    y, xl = q // 2, q % 2
    return xl * 8 + y // 2 % 2 * 4 + y // 4 * 2 + y % 2


SLOT = [slot_of(q) for q in range(16)]
FIRST = sorted(SLOT[:8])


def kernel(a_hbm, v_hbm, t_hbm, upd_ref, a_ref, v_ref, t_ref, ah, al, vh, vl, pt, rs_recv, zx_recv, zcol, vcol,
           zrow, s21, gloc, ga_recv, gtiles, gc_recv, gfull, qh, ql, uh, ul, yt1_ref, load_sems, send_sems, recv_sems):
    width = v_ref.shape[1]
    cols = a_ref.shape[1]
    nb = width // 2
    sub = width // 16
    vsub = cols // 16
    half = sub // 2
    r = lax.axis_index("prow")
    c = lax.axis_index("pcol")
    y, xl = r // 2, r % 2
    chip, k = c // 2, c % 2
    xh, z = chip // 8, chip % 8
    y2, y1, y0 = y // 4, y // 2 % 2, y % 2
    z2, z1, z0 = z // 4, z // 2 % 2, z % 2

    y_peers = [((y + o) % RING * 2 + xl, c) for o in range(1, RING)]
    y_up, y_down = y_peers[0], y_peers[-1]
    z_up = (r, (xh * 8 + (z + 1) % RING) * 2 + k)
    z_down = (r, (xh * 8 + (z + RING - 1) % RING) * 2 + k)
    x_near = (y * 2 + 1 - xl, c)
    x_far = (r, ((1 - xh) * 8 + z) * 2 + k)
    other = (r, chip * 2 + 1 - k)
    x_other = (y * 2 + 1 - xl, chip * 2 + 1 - k)
    v_from = (chip, (xl * 8 + (y2 + z0) % 2 * 4 + (y1 + z1) % 2 * 2 + y0) * 2 + k)
    v_piece = (z2 + xl) % 2 * 4 + (z1 + y0) % 2 * 2 + z0
    v_to = (v_piece * 2 + xh, r * 2 + k)
    v_apart = jnp.logical_or(v_to[0] != r, v_to[1] != c)
    q = (z1 * 4 + z2 * 2 + z0) * 2 + xh
    z_to = (chip, (xl * 8 + y1 * 4 + y2 * 2 + y0) * 2 + k)
    z_from = (q, r * 2 + k)
    z_apart = jnp.logical_or(z_to[0] != r, z_to[1] != c)

    count = [0]
    started = []

    def copy(src, dst, device):
        slot = count[0]
        count[0] += 1
        return pltpu.make_async_remote_copy(
            src_ref=src, dst_ref=dst, send_sem=send_sems.at[slot], recv_sem=recv_sems.at[slot],
            device_id=device, device_id_type=pl.DeviceIdType.MESH)

    def go(op):
        op.start()
        started.append(op)
        return op

    barrier = pltpu.get_barrier_semaphore()

    def greet(device):
        pl.semaphore_signal(barrier, inc=1, device_id=device, device_id_type=pl.DeviceIdType.MESH)

    fixed = [*y_peers, x_near, x_other, z_up, z_down, x_far, other]
    for device in fixed:
        greet(device)

    @pl.when(v_apart)
    def _():
        greet(v_from)

    @pl.when(z_apart)
    def _():
        greet(z_from)

    loads = [pltpu.make_async_copy(src, dst, load_sems.at[i])
             for i, (src, dst) in enumerate(((v_hbm, v_ref), (a_hbm, a_ref), (t_hbm, t_ref)))]
    for load in loads:
        load.start()
    loads[0].wait()
    vh[...], vl[...] = split(v_ref[...])
    loads[1].wait()
    ah[...], al[...] = split(a_ref[...])

    def product(group):
        lanes = pl.ds(pl.multiple_of((group + 4) % 4 * 128, 128), 128)
        pt[lanes, :] = dot3((vh[:, lanes], vl[:, lanes]), (ah[...], al[...]), TN)

    far_group, side = (y + 4) // 2, 1 - 2 * ((y + 1) % 2)
    product(far_group)
    product(far_group + side)

    pl.semaphore_wait(barrier, len(fixed) + v_apart.astype(jnp.int32) + z_apart.astype(jnp.int32))

    def pt_at(part, index):
        return pl.ds(pl.multiple_of((index + RING) % RING * (2 * sub) + part * sub, sub), sub)

    NAMES = ("RA", "LB", "RB", "LA")
    first = {"RA": 0, "LB": 0, "RB": 1, "LA": 1}
    base = {"RA": 0, "LB": 4, "RB": 7, "LA": 10}
    rs = {}

    def rs_at(name, s):
        return pt_at(0 if name[1] == "A" else 1, y + 4 - s if name[0] == "R" else y - 4 + s)

    def rs_send(name, s):
        rs[name, s] = go(copy(pt.at[rs_at(name, s), :], rs_recv.at[base[name] + s], y_up if name[0] == "R" else y_down))

    def rs_round(s):
        for name in NAMES:
            if s - 1 >= first[name]:
                rs[name, s - 1].wait_recv()
                at = rs_at(name, s)
                pt[at, :] = pt[at, :] + rs_recv[base[name] + s - 1]
                rs_send(name, s)

    for name in NAMES:
        rs_send(name, first[name])

    v_rows = pl.ds(pl.multiple_of(v_piece * 2 * vsub, 8), 2 * vsub)
    v_src = pl.ds(pl.multiple_of(k * cols + v_piece * 2 * vsub, 8), 2 * vsub)
    v_copy = copy(v_ref.at[v_src, :], vcol.at[v_rows, :], v_to)

    @pl.when(v_apart)
    def _():
        v_copy.start()

    @pl.when(jnp.logical_not(v_apart))
    def _():
        vcol[v_rows, :] = v_ref[v_src, :]

    product(far_group - side)
    rs_round(1)
    product(far_group + 2)
    rs_round(2)

    half_rows = pl.ds(pl.multiple_of(k * cols, 128), cols)
    s21[...] = dot3((vh[half_rows, nb:], vl[half_rows, nb:]), (vh[half_rows, :nb], vl[half_rows, :nb]), TN)
    rs_round(3)

    def ring(ref_of, me, up, down):
        ops = {}
        last = {"RA": 3, "LB": 3, "RB": 2, "LA": 2}

        def step(s, arrived=None):
            for name in NAMES:
                part = 0 if name[1] == "A" else 1
                index = (me - s + RING) % RING if name[0] == "R" else (me + s) % RING
                if s >= 1 and s - 1 <= last[name]:
                    ops[name, s - 1].wait_recv()
                if s <= last[name]:
                    ref = ref_of(part, index)
                    ops[name, s] = go(copy(ref, ref, up if name[0] == "R" else down))
                if arrived is not None and s >= 1 and s - 1 <= last[name]:
                    arrived(part, index)
        return step

    def zrow_at(core, h, i):
        return zrow.at[core, pl.ds(pl.multiple_of((h * 8 + i) * sub, sub), sub), :]

    v_ring = ring(lambda h, i: vcol.at[pl.ds(pl.multiple_of(i * 2 * vsub + h * vsub, 8), vsub), :], y, y_up, y_down)
    z_ring = ring(lambda h, i: zcol.at[pt_at(h, i), :], y, y_up, y_down)
    row_ring = ring(lambda h, i: zrow_at(k, h, i), z, z_up, z_down)
    g_ring = ring(lambda h, i: gfull.at[(h * 8 + i) * 2 + k], z, z_up, z_down)
    rows_over, g_over = [], []

    def pass_row(h, i):
        rows_over.append(go(copy(zrow_at(k, h, i), zrow_at(k, h, i), other)))

    def pass_g(h, i):
        ref = gfull.at[(h * 8 + i) * 2 + k]
        g_over.append(go(copy(ref, ref, other)))

    @pl.when(v_apart)
    def _():
        v_copy.wait_recv()

    v_ring(0)
    for part, names in ((0, ("RA", "LA")), (1, ("LB", "RB"))):
        at = pt_at(part, y)
        total = pt[at, :]
        for name in names:
            rs[name, 3].wait_recv()
            total = total + rs_recv[base[name] + 3]
        pt[at, :] = total

    def zx_at(part):
        return pl.ds(pl.multiple_of(part * sub, sub), sub)

    x_ops = [go(copy(pt.at[pt_at(part, y), :], zx_recv.at[zx_at(part), :], x_near)) for part in (1 - xl, xl)]
    v_ring(1)

    own, rest = pt_at(xl, y), pt_at(1 - xl, y)
    x_ops[0].wait_recv()
    zcol[own, :] = pt[own, :] + zx_recv[zx_at(xl), :]
    z_rows = pl.ds(pl.multiple_of((z_to[1] // 2) * sub, sub), sub)
    z_copy = copy(zcol.at[own, :], zrow.at[k, z_rows, :], z_to)

    @pl.when(z_apart)
    def _():
        z_copy.start()

    @pl.when(jnp.logical_not(z_apart))
    def _():
        zrow[k, z_rows, :] = zcol[own, :]

    x_ops[1].wait_recv()
    zcol[rest, :] = pt[rest, :] + zx_recv[zx_at(1 - xl), :]
    z_ring(0)
    v_ring(2)

    @pl.when(z_apart)
    def _():
        z_copy.wait_recv()

    mine = zrow_at(k, xh, z)
    part = dot3(split(zrow[k, pl.ds(pl.multiple_of(chip * sub, sub), sub), :]), (vh[half_rows, :], vl[half_rows, :]), NN)
    s_rows = s21[pl.ds(pl.multiple_of(q % 8 * sub, sub), sub), :]
    gloc[:, :nb] = jnp.where(q >= 8, s_rows, part[:, :nb])
    gloc[:, nb:] = part[:, nb:]
    my_half = pl.ds(pl.multiple_of(k * half, half), half)
    its_half = pl.ds(pl.multiple_of((1 - k) * half, half), half)
    ga = [go(copy(gloc.at[its_half, :], ga_recv.at[0], x_other)),
          go(copy(gloc.at[my_half, :], ga_recv.at[1], x_near)),
          go(copy(gloc.at[its_half, :], ga_recv.at[2], other))]
    far_op = go(copy(mine, mine, x_far))
    pass_row(xh, z)
    z_ring(1)
    total = gloc[my_half, :]
    for i in (2, 1, 0):
        ga[i].wait_recv()
        total = total + ga_recv[i]
    for j in range(8):
        gtiles[j] = total[j // 4 * 8:j // 4 * 8 + 8, j % 4 * 128:(j % 4 + 1) * 128]
    gc = [go(copy(gtiles.at[(y + o) % RING], gc_recv.at[o], y_peers[o - 1])) for o in range(1, RING)]
    far_op.wait_recv()
    row_ring(0)
    pass_row(1 - xh, z)
    v_ring(3)
    tile = gtiles[y]
    for o in range(1, RING):
        gc[o - 1].wait_recv()
        tile = tile + gc_recv[o]
    gfull[c, y] = tile
    gd = [go(copy(gfull.at[c, y], gfull.at[c, y], y_peers[o - 1])) for o in range(1, RING)]
    z_ring(2)
    v_ring(4)

    loads[2].wait()
    t1, t2 = split(t_ref[0]), split(t_ref[1])
    v1, v2 = split(vcol[:, :nb]), split(vcol[:, nb:])
    for p, (t, v) in enumerate(((t1, v1), (t2, v2))):
        u_high, u_low = split(dot3(t, v, NT))
        for i in range(8):
            at = SLOT[p * 8 + i] * sub
            uh[at:at + sub, :] = u_high[i * sub:(i + 1) * sub, :]
            ul[at:at + sub, :] = u_low[i * sub:(i + 1) * sub, :]
    for op in gd:
        op.wait_recv()
    ge = go(copy(gfull.at[c], gfull.at[c], x_far))
    pass_g(xh, z)
    row_ring(1, pass_row)
    z_ring(3)
    ge.wait_recv()
    g_ring(0)
    pass_g(1 - xh, z)
    row_ring(2, pass_row)
    z_ring(4)
    yt1 = dot3(t1, split(zcol[:nb, :]), TN)
    yt1_ref[...] = yt1
    qh[:nb, :], ql[:nb, :] = split(yt1)
    qh[nb:, :], ql[nb:, :] = split(dot3(t2, split(zcol[nb:, :]), TN))
    g_ring(1, pass_g)
    row_ring(3, pass_row)
    row_ring(4, pass_row)
    g_ring(2, pass_g)
    for op in rows_over:
        op.wait_recv()

    def tiles(i):
        for h in range(2):
            at = pl.ds(pl.multiple_of(h * cols + i * 128, 128), 128)
            yield h, at, pl.ds(pl.multiple_of(i * 128, 128), 128)

    def early(i, _):
        for h, at, lanes in tiles(i):
            acc = dot3((vh[at, :], vl[at, :]), (qh[...], ql[...]), NN)
            upd_ref[at, :] = -acc - dot3(split(zrow[h, :, lanes]), (uh[...], ul[...]), TN)
        return 0

    def late(i, _):
        for h, at, lanes in tiles(i):
            acc = dot3((vh[at, :], vl[at, :]), (qh[...], ql[...]), NN)
            kept = jnp.concatenate([zrow[h, s * sub:(s + 1) * sub, lanes] for s in FIRST], axis=0)
            upd_ref[at, :] = upd_ref[at, :] - acc - dot3(split(kept), (uh[:nb, :], ul[:nb, :]), TN)
        return 0

    lax.fori_loop(0, 2, early, 0)
    g_ring(3, pass_g)
    lax.fori_loop(2, 3, early, 0)
    g_ring(4, pass_g)
    for op in g_over:
        op.wait_recv()

    def block(row, col):
        lanes = []
        for j in (2 * col, 2 * col + 1):
            found = [gfull[SLOT[i] * 2 + core, h * 4 + j]
                     for i in range(row * 8, row * 8 + 8) for core in range(2) for h in range(2)]
            lanes.append(jnp.concatenate(found, axis=0))
        return jnp.concatenate(lanes, axis=1)

    g11, g12, s_21, g22 = block(0, 0), block(0, 1), block(1, 0), block(1, 1)
    s_21s = split(s_21)
    s_12s = split(s_21.T)
    e = dot3(s_12s, t2, NN)
    es = split(e)
    m1 = dot3(t1, split(dot3(split(g11), t1, NN)), TN)
    m1s = split(m1)
    kk = dot3(t1, split(g12), TN) - 0.5 * dot3(m1s, s_12s, TN)
    kks = split(kk)
    jj = dot3(s_21s, kks, NN)
    m2 = dot3(t2, split(dot3(split(g22 - jj - jj.T), t2, NN)), TN)
    h12s = split(0.5 * dot3(m1s, es, NN) - dot3(kks, t2, NN))
    qh[:nb, :], ql[:nb, :] = split(dot3(h12s, v2, NT) - dot3(m1s, v1, NT))
    low_q = dot3(h12s, v1, (((0,), (1,)), ((), ()))) - dot3(split(m2), v2, NT)
    qh[nb:, :], ql[nb:, :] = split(low_q - dot3(es, split(yt1_ref[...]), TN))
    u_high, u_low = split(-dot3(t1, split(dot3(es, v2, NT)), NN))
    for at, s in enumerate(FIRST):
        i = SLOT.index(s)
        uh[at * sub:(at + 1) * sub, :] = u_high[i * sub:(i + 1) * sub, :]
        ul[at * sub:(at + 1) * sub, :] = u_low[i * sub:(i + 1) * sub, :]
    lax.fori_loop(0, cols // 128, late, 0)

    for op in started:
        op.wait_send()

    @pl.when(v_apart)
    def _():
        v_copy.wait_send()

    @pl.when(z_apart)
    def _():
        z_copy.wait_send()


COPIES = 14 + 2 + 2 + 14 + 14 + (1 + 14 + 16) + (3 + 7 + 7 + 1 + 14 + 16)


def body(matrix, reflectors, factors):
    rows, cols = matrix.shape
    width = reflectors.shape[1]
    nb = width // 2
    sub = width // 16
    vmem = pl.BlockSpec(memory_space=pltpu.VMEM)
    update = pl.pallas_call(
        kernel,
        out_shape=jax.ShapeDtypeStruct((rows, cols), F32),
        in_specs=[pl.BlockSpec(memory_space=pltpu.HBM)] * 3,
        out_specs=vmem,
        scratch_shapes=[
            pltpu.VMEM((rows, cols), F32),
            pltpu.VMEM((rows, width), F32),
            pltpu.VMEM(factors.shape, F32),
            pltpu.VMEM((rows, cols), BF16),
            pltpu.VMEM((rows, cols), BF16),
            pltpu.VMEM((rows, width), BF16),
            pltpu.VMEM((rows, width), BF16),
            pltpu.VMEM((width, cols), F32),
            pltpu.VMEM((14, sub, cols), F32),
            pltpu.VMEM((2 * sub, cols), F32),
            pltpu.VMEM((width, cols), F32),
            pltpu.VMEM((cols, width), F32),
            pltpu.VMEM((2, width, cols), F32),
            pltpu.VMEM((nb, nb), F32),
            pltpu.VMEM((sub, width), F32),
            pltpu.VMEM((3, sub // 2, width), F32),
            pltpu.VMEM((8, 8, 128), F32),
            pltpu.VMEM((8, 8, 128), F32),
            pltpu.VMEM((32, 8, 8, 128), F32),
            pltpu.VMEM((width, cols), BF16),
            pltpu.VMEM((width, cols), BF16),
            pltpu.VMEM((width, cols), BF16),
            pltpu.VMEM((width, cols), BF16),
            pltpu.VMEM((nb, cols), F32),
            pltpu.SemaphoreType.DMA((3,)),
            pltpu.SemaphoreType.DMA((COPIES,)),
            pltpu.SemaphoreType.DMA((COPIES,)),
        ],
        compiler_params=pltpu.CompilerParams(
            collective_id=0, has_side_effects=True, vmem_limit_bytes=60 * 1024 * 1024),
        name="two_panels",
    )(matrix, reflectors, factors)
    return matrix + update


def solution(mesh):
    return jax.shard_map(
        body,
        mesh=mesh,
        in_specs=(P("prow", "pcol"), P("prow", None), P()),
        out_specs=P("prow", "pcol"),
        check_vma=False,
    )
```

```python
import jax
import jax.numpy as jnp
from jax import lax
from jax.experimental import pallas as pl
from jax.experimental.pallas import tpu as pltpu
from jax.sharding import PartitionSpec as P

F32 = jnp.float32
BF16 = jnp.bfloat16
RING = 8
NN = (((1,), (0,)), ((), ()))
TN = (((0,), (0,)), ((), ()))
NT = (((1,), (1,)), ((), ()))


def split(x):
    high = x.astype(BF16)
    return high, (x - high.astype(F32)).astype(BF16)


def dot3(left, right, dims):
    (lh, ll), (rh, rl) = left, right
    def one(p, q):
        return lax.dot_general(p, q, dims, preferred_element_type=F32)
    return one(lh, rh) + (one(lh, rl) + one(ll, rh))


def mm(left, right, dims):
    return dot3(split(left), split(right), dims)


def slot_of(q):
    y, xl = q // 2, q % 2
    return (y // 2 % 2 * 4 + y // 4 * 2 + y % 2) * 2 + xl


SLOT = [slot_of(q) for q in range(16)]
FIRST = sorted(SLOT[:8])


def kernel(a_hbm, v_hbm, t_hbm, upd_ref, a_ref, v_ref, t_ref, ah, al, vh, vl, pt, rs_recv, zx_recv, zcol, vcol,
           zrow, s21, gloc, ga_recv, gtiles, gc_recv, gfull, qh, ql, uh, ul, yt1_ref, load_sems, send_sems, recv_sems):
    width = v_ref.shape[1]
    cols = a_ref.shape[1]
    nb = width // 2
    sub = width // 16
    vsub = cols // 16
    half = sub // 2
    r = lax.axis_index("prow")
    c = lax.axis_index("pcol")
    y, xl = r // 2, r % 2
    chip, k = c // 2, c % 2
    xh, z = chip // 8, chip % 8
    y2, y1, y0 = y // 4, y // 2 % 2, y % 2
    z2, z1, z0 = z // 4, z // 2 % 2, z % 2

    y_peers = [((y + o) % RING * 2 + xl, c) for o in range(1, RING)]
    y_up, y_down = y_peers[0], y_peers[-1]
    mine = z * 2 + xh
    y_at = {1: y_peers[0], 2: y_peers[1], -2: y_peers[-2], -1: y_peers[-1]}
    z_at = {o: (r, (xh * 8 + (z + o + RING) % RING) * 2 + k) for o in (1, 2, -2, -1)}
    x_near = (y * 2 + 1 - xl, c)
    x_far = (r, ((1 - xh) * 8 + z) * 2 + k)
    other = (r, chip * 2 + 1 - k)
    x_other = (y * 2 + 1 - xl, chip * 2 + 1 - k)
    v_from = (chip, (xl * 8 + (y2 + z0) % 2 * 4 + (y1 + z1) % 2 * 2 + y0) * 2 + k)
    v_piece = (z2 + xl) % 2 * 4 + (z1 + y0) % 2 * 2 + z0
    v_to = (v_piece * 2 + xh, r * 2 + k)
    v_apart = jnp.logical_or(v_to[0] != r, v_to[1] != c)
    q = (z1 * 4 + z2 * 2 + z0) * 2 + xh
    z_to = (chip, (xl * 8 + y1 * 4 + y2 * 2 + y0) * 2 + k)
    z_from = (q, r * 2 + k)
    z_apart = jnp.logical_or(z_to[0] != r, z_to[1] != c)

    count = [0]
    started = []

    def copy(src, dst, device):
        slot = count[0]
        count[0] += 1
        return pltpu.make_async_remote_copy(
            src_ref=src, dst_ref=dst, send_sem=send_sems.at[slot], recv_sem=recv_sems.at[slot],
            device_id=device, device_id_type=pl.DeviceIdType.MESH)

    def go(op):
        op.start()
        started.append(op)
        return op

    barrier = pltpu.get_barrier_semaphore()

    def greet(device):
        pl.semaphore_signal(barrier, inc=1, device_id=device, device_id_type=pl.DeviceIdType.MESH)

    fixed = [*y_peers, x_near, x_other, *z_at.values(), x_far, other]
    for device in fixed:
        greet(device)

    @pl.when(v_apart)
    def _():
        greet(v_from)

    @pl.when(z_apart)
    def _():
        greet(z_from)

    loads = [pltpu.make_async_copy(src, dst, load_sems.at[i])
             for i, (src, dst) in enumerate(((v_hbm, v_ref), (a_hbm, a_ref), (t_hbm, t_ref)))]
    for load in loads:
        load.start()
    loads[0].wait()
    vh[...], vl[...] = split(v_ref[...])
    loads[1].wait()
    ah[...], al[...] = split(a_ref[...])

    def product(group):
        lanes = pl.ds(pl.multiple_of((group + 4) % 4 * 128, 128), 128)
        pt[lanes, :] = dot3((vh[:, lanes], vl[:, lanes]), (ah[...], al[...]), TN)

    far_group, side = (y + 4) // 2, 1 - 2 * ((y + 1) % 2)
    product(far_group)
    product(far_group + side)

    pl.semaphore_wait(barrier, len(fixed) + v_apart.astype(jnp.int32) + z_apart.astype(jnp.int32))

    def pt_at(part, index):
        return pl.ds(pl.multiple_of((index + RING) % RING * (2 * sub) + part * sub, sub), sub)

    NAMES = ("RA", "LB", "RB", "LA")
    first = {"RA": 0, "LB": 0, "RB": 1, "LA": 1}
    base = {"RA": 0, "LB": 4, "RB": 7, "LA": 10}
    rs = {}

    def rs_at(name, s):
        return pt_at(0 if name[1] == "A" else 1, y + 4 - s if name[0] == "R" else y - 4 + s)

    def rs_send(name, s):
        rs[name, s] = go(copy(pt.at[rs_at(name, s), :], rs_recv.at[base[name] + s], y_up if name[0] == "R" else y_down))

    def rs_round(s):
        for name in NAMES:
            if s - 1 >= first[name]:
                rs[name, s - 1].wait_recv()
                at = rs_at(name, s)
                pt[at, :] = pt[at, :] + rs_recv[base[name] + s - 1]
                rs_send(name, s)

    for name in NAMES:
        rs_send(name, first[name])

    v_rows = pl.ds(pl.multiple_of(v_piece * 2 * vsub, 8), 2 * vsub)
    v_src = pl.ds(pl.multiple_of(k * cols + v_piece * 2 * vsub, 8), 2 * vsub)
    v_copy = copy(v_ref.at[v_src, :], vcol.at[v_rows, :], v_to)

    @pl.when(v_apart)
    def _():
        v_copy.start()

    @pl.when(jnp.logical_not(v_apart))
    def _():
        vcol[v_rows, :] = v_ref[v_src, :]

    product(far_group - side)
    rs_round(1)
    product(far_group + 2)
    rs_round(2)

    half_rows = pl.ds(pl.multiple_of(k * cols, 128), cols)
    s21[...] = dot3((vh[half_rows, nb:], vl[half_rows, nb:]), (vh[half_rows, :nb], vl[half_rows, :nb]), TN)
    rs_round(3)

    def gather(whole, halves, me, at):
        ops = {}

        def near():
            for o in (1, -1, 2, -2):
                ops[o] = go(copy(whole(me), whole(me), at[o]))

        def on():
            for o in (2, -2):
                ops[o].wait_recv()
                index = (me - o + RING) % RING
                half_ref = halves(0 if o > 0 else 1, index)
                ops[o, 1] = go(copy(whole(index), whole(index), at[o // 2]))
                ops[o, 2] = go(copy(half_ref, half_ref, at[o]))

        def last():
            for o in (2, -2):
                ops[o // 2].wait_recv()
                ops[o, 1].wait_recv()
                ops[o, 2].wait_recv()

        return near, on, last

    def slots(index):
        return pl.ds(pl.multiple_of(index * 2 * sub, sub), 2 * sub)

    def row_chunk(index):
        return zrow.at[k, slots(index), :]

    def row_half(part, index):
        return zrow.at[k, pl.ds(pl.multiple_of(index * 2 * sub + part * sub, sub), sub), :]

    def g_chunk(index):
        return gfull.at[k, pl.ds(index * 2, 2)]

    def v_rows_of(start, size):
        return vcol.at[pl.ds(pl.multiple_of(start, 8), size), :]

    v_gather = gather(lambda i: v_rows_of(i * 2 * vsub, 2 * vsub),
                      lambda h, i: v_rows_of(i * 2 * vsub + h * vsub, vsub), y, y_at)
    z_gather = gather(lambda i: zcol.at[slots(i), :], lambda h, i: zcol.at[pt_at(h, i), :], y, y_at)
    row_gather = gather(row_chunk, row_half, z, z_at)
    g_gather = gather(g_chunk, lambda h, i: gfull.at[k, pl.ds(i * 2 + h, 1)], z, z_at)
    over = {row_chunk: [], g_chunk: []}

    def pass_on(chunk, offsets):
        for o in offsets:
            ref = chunk((z + o + RING) % RING)
            over[chunk].append(go(copy(ref, ref, other)))

    @pl.when(v_apart)
    def _():
        v_copy.wait_recv()

    v_gather[0]()
    for part, names in ((0, ("RA", "LA")), (1, ("LB", "RB"))):
        at = pt_at(part, y)
        total = pt[at, :]
        for name in names:
            rs[name, 3].wait_recv()
            total = total + rs_recv[base[name] + 3]
        pt[at, :] = total

    def zx_at(part):
        return pl.ds(pl.multiple_of(part * sub, sub), sub)

    x_ops = [go(copy(pt.at[pt_at(part, y), :], zx_recv.at[zx_at(part), :], x_near)) for part in (1 - xl, xl)]
    v_gather[1]()

    own, rest = pt_at(xl, y), pt_at(1 - xl, y)
    x_ops[0].wait_recv()
    zcol[own, :] = pt[own, :] + zx_recv[zx_at(xl), :]
    z_rows = pl.ds(pl.multiple_of(((y1 * 4 + y2 * 2 + y0) * 2 + xl) * sub, sub), sub)
    z_copy = copy(zcol.at[own, :], zrow.at[k, z_rows, :], z_to)

    @pl.when(z_apart)
    def _():
        z_copy.start()

    @pl.when(jnp.logical_not(z_apart))
    def _():
        zrow[k, z_rows, :] = zcol[own, :]

    x_ops[1].wait_recv()
    zcol[rest, :] = pt[rest, :] + zx_recv[zx_at(1 - xl), :]
    z_gather[0]()

    @pl.when(z_apart)
    def _():
        z_copy.wait_recv()

    own_slot = pl.ds(pl.multiple_of(mine * sub, sub), sub)
    part = dot3(split(zrow[k, own_slot, :]), (vh[half_rows, :], vl[half_rows, :]), NN)
    s_rows = s21[pl.ds(pl.multiple_of(q % 8 * sub, sub), sub), :]
    gloc[:, :nb] = jnp.where(q >= 8, s_rows, part[:, :nb])
    gloc[:, nb:] = part[:, nb:]
    my_half = pl.ds(pl.multiple_of(k * half, half), half)
    its_half = pl.ds(pl.multiple_of((1 - k) * half, half), half)
    ga = [go(copy(gloc.at[its_half, :], ga_recv.at[0], x_other)),
          go(copy(gloc.at[my_half, :], ga_recv.at[1], x_near)),
          go(copy(gloc.at[its_half, :], ga_recv.at[2], other))]
    far_op = go(copy(zrow.at[k, own_slot, :], zrow.at[k, own_slot, :], x_far))
    z_gather[1]()
    total = gloc[my_half, :]
    for i in (2, 1, 0):
        ga[i].wait_recv()
        total = total + ga_recv[i]
    for j in range(8):
        gtiles[j] = total[j // 4 * 8:j // 4 * 8 + 8, j % 4 * 128:(j % 4 + 1) * 128]
    gc = [go(copy(gtiles.at[(y + o) % RING], gc_recv.at[o], y_peers[o - 1])) for o in range(1, RING)]
    far_op.wait_recv()
    row_gather[0]()
    pass_on(row_chunk, (0,))
    tile = gtiles[y]
    for o in range(1, RING):
        gc[o - 1].wait_recv()
        tile = tile + gc_recv[o]
    gfull[k, mine, y] = tile
    gd = [go(copy(gfull.at[k, mine, y], gfull.at[k, mine, y], y_peers[o - 1])) for o in range(1, RING)]
    row_gather[1]()
    pass_on(row_chunk, (2, -2))
    v_gather[2]()

    loads[2].wait()
    t1, t2 = split(t_ref[0]), split(t_ref[1])
    v1, v2 = split(vcol[:, :nb]), split(vcol[:, nb:])
    for p, (t, v) in enumerate(((t1, v1), (t2, v2))):
        u_high, u_low = split(dot3(t, v, NT))
        for i in range(8):
            at = SLOT[p * 8 + i] * sub
            uh[at:at + sub, :] = u_high[i * sub:(i + 1) * sub, :]
            ul[at:at + sub, :] = u_low[i * sub:(i + 1) * sub, :]
    for op in gd:
        op.wait_recv()
    ge = go(copy(gfull.at[k, mine], gfull.at[k, mine], x_far))
    row_gather[2]()
    pass_on(row_chunk, (1, -1, 3, -3, 4))
    z_gather[2]()
    ge.wait_recv()
    g_gather[0]()
    pass_on(g_chunk, (0,))
    yt1 = dot3(t1, split(zcol[:nb, :]), TN)
    yt1_ref[...] = yt1
    qh[:nb, :], ql[:nb, :] = split(yt1)
    qh[nb:, :], ql[nb:, :] = split(dot3(t2, split(zcol[nb:, :]), TN))
    for op in over[row_chunk]:
        op.wait_recv()

    def tiles(i):
        for h in range(2):
            at = pl.ds(pl.multiple_of(h * cols + i * 128, 128), 128)
            yield h, at, pl.ds(pl.multiple_of(i * 128, 128), 128)

    def early(i, _):
        for h, at, lanes in tiles(i):
            acc = dot3((vh[at, :], vl[at, :]), (qh[...], ql[...]), NN)
            upd_ref[at, :] = -acc - dot3(split(zrow[h, :, lanes]), (uh[...], ul[...]), TN)
        return 0

    def late(i, _):
        for h, at, lanes in tiles(i):
            acc = dot3((vh[at, :], vl[at, :]), (qh[...], ql[...]), NN)
            kept = jnp.concatenate([zrow[h, s * sub:(s + 1) * sub, lanes] for s in FIRST], axis=0)
            upd_ref[at, :] = upd_ref[at, :] - acc - dot3(split(kept), (uh[:nb, :], ul[:nb, :]), TN)
        return 0

    lax.fori_loop(0, 1, early, 0)
    g_gather[1]()
    pass_on(g_chunk, (2, -2))
    lax.fori_loop(1, 3, early, 0)
    g_gather[2]()
    pass_on(g_chunk, (1, -1, 3, -3, 4))
    for op in over[g_chunk]:
        op.wait_recv()

    def block(row, col):
        lanes = []
        for j in (2 * col, 2 * col + 1):
            found = [gfull[core, SLOT[i], h * 4 + j]
                     for i in range(row * 8, row * 8 + 8) for core in range(2) for h in range(2)]
            lanes.append(jnp.concatenate(found, axis=0))
        return jnp.concatenate(lanes, axis=1)

    g11, g12, s_21, g22 = block(0, 0), block(0, 1), block(1, 0), block(1, 1)
    s_21s = split(s_21)
    s_12s = split(s_21.T)
    e = dot3(s_12s, t2, NN)
    es = split(e)
    m1 = dot3(t1, split(dot3(split(g11), t1, NN)), TN)
    m1s = split(m1)
    kk = dot3(t1, split(g12), TN) - 0.5 * dot3(m1s, s_12s, TN)
    kks = split(kk)
    jj = dot3(s_21s, kks, NN)
    m2 = dot3(t2, split(dot3(split(g22 - jj - jj.T), t2, NN)), TN)
    h12s = split(0.5 * dot3(m1s, es, NN) - dot3(kks, t2, NN))
    qh[:nb, :], ql[:nb, :] = split(dot3(h12s, v2, NT) - dot3(m1s, v1, NT))
    low_q = dot3(h12s, v1, (((0,), (1,)), ((), ()))) - dot3(split(m2), v2, NT)
    qh[nb:, :], ql[nb:, :] = split(low_q - dot3(es, split(yt1_ref[...]), TN))
    u_high, u_low = split(-dot3(t1, split(dot3(es, v2, NT)), NN))
    for at, s in enumerate(FIRST):
        i = SLOT.index(s)
        uh[at * sub:(at + 1) * sub, :] = u_high[i * sub:(i + 1) * sub, :]
        ul[at * sub:(at + 1) * sub, :] = u_low[i * sub:(i + 1) * sub, :]
    lax.fori_loop(0, cols // 128, late, 0)

    for op in started:
        op.wait_send()

    @pl.when(v_apart)
    def _():
        v_copy.wait_send()

    @pl.when(z_apart)
    def _():
        z_copy.wait_send()


COPIES = 14 + 2 + 2 + 8 + 8 + (1 + 8 + 8) + (3 + 7 + 7 + 1 + 8 + 8)


def body(matrix, reflectors, factors):
    rows, cols = matrix.shape
    width = reflectors.shape[1]
    nb = width // 2
    sub = width // 16
    vmem = pl.BlockSpec(memory_space=pltpu.VMEM)
    update = pl.pallas_call(
        kernel,
        out_shape=jax.ShapeDtypeStruct((rows, cols), F32),
        in_specs=[pl.BlockSpec(memory_space=pltpu.HBM)] * 3,
        out_specs=vmem,
        scratch_shapes=[
            pltpu.VMEM((rows, cols), F32),
            pltpu.VMEM((rows, width), F32),
            pltpu.VMEM(factors.shape, F32),
            pltpu.VMEM((rows, cols), BF16),
            pltpu.VMEM((rows, cols), BF16),
            pltpu.VMEM((rows, width), BF16),
            pltpu.VMEM((rows, width), BF16),
            pltpu.VMEM((width, cols), F32),
            pltpu.VMEM((14, sub, cols), F32),
            pltpu.VMEM((2 * sub, cols), F32),
            pltpu.VMEM((width, cols), F32),
            pltpu.VMEM((cols, width), F32),
            pltpu.VMEM((2, width, cols), F32),
            pltpu.VMEM((nb, nb), F32),
            pltpu.VMEM((sub, width), F32),
            pltpu.VMEM((3, sub // 2, width), F32),
            pltpu.VMEM((8, 8, 128), F32),
            pltpu.VMEM((8, 8, 128), F32),
            pltpu.VMEM((2, 16, 8, 8, 128), F32),
            pltpu.VMEM((width, cols), BF16),
            pltpu.VMEM((width, cols), BF16),
            pltpu.VMEM((width, cols), BF16),
            pltpu.VMEM((width, cols), BF16),
            pltpu.VMEM((nb, cols), F32),
            pltpu.SemaphoreType.DMA((3,)),
            pltpu.SemaphoreType.DMA((COPIES,)),
            pltpu.SemaphoreType.DMA((COPIES,)),
        ],
        compiler_params=pltpu.CompilerParams(
            collective_id=0, has_side_effects=True, vmem_limit_bytes=60 * 1024 * 1024),
        name="two_panels",
    )(matrix, reflectors, factors)
    return matrix + update


def solution(mesh):
    return jax.shard_map(
        body,
        mesh=mesh,
        in_specs=(P("prow", "pcol"), P("prow", None), P()),
        out_specs=P("prow", "pcol"),
        check_vma=False,
    )
```

```python
import jax
import jax.numpy as jnp
from jax import lax
from jax.experimental import pallas as pl
from jax.experimental.pallas import tpu as pltpu
from jax.sharding import PartitionSpec as P

F32 = jnp.float32
BF16 = jnp.bfloat16
RING = 8
NN = (((1,), (0,)), ((), ()))
TN = (((0,), (0,)), ((), ()))
NT = (((1,), (1,)), ((), ()))


def split(x):
    high = x.astype(BF16)
    return high, (x - high.astype(F32)).astype(BF16)


def dot3(left, right, dims):
    (lh, ll), (rh, rl) = left, right
    def one(p, q):
        return lax.dot_general(p, q, dims, preferred_element_type=F32)
    return one(lh, rh) + (one(lh, rl) + one(ll, rh))


def mm(left, right, dims):
    return dot3(split(left), split(right), dims)


def slot_of(q):
    y, xl = q // 2, q % 2
    return (y // 2 % 2 * 4 + y // 4 * 2 + y % 2) * 2 + xl


SLOT = [slot_of(q) for q in range(16)]
FIRST = sorted(SLOT[:8])


def kernel(a_hbm, v_hbm, t_hbm, upd_ref, a_ref, v_ref, t_ref, ah, al, vh, vl, pt, rs_recv, zx_recv, zcol, vcol,
           zrow, s21, gloc, ga_recv, gtiles, gc_recv, gfull, qh, ql, uh, ul, yt1_ref, load_sems, send_sems, recv_sems):
    width = v_ref.shape[1]
    cols = a_ref.shape[1]
    nb = width // 2
    sub = width // 16
    vsub = cols // 16
    half = sub // 2
    r = lax.axis_index("prow")
    c = lax.axis_index("pcol")
    y, xl = r // 2, r % 2
    chip, k = c // 2, c % 2
    xh, z = chip // 8, chip % 8
    y2, y1, y0 = y // 4, y // 2 % 2, y % 2
    z2, z1, z0 = z // 4, z // 2 % 2, z % 2

    y_peers = [((y + o) % RING * 2 + xl, c) for o in range(1, RING)]
    y_up, y_down = y_peers[0], y_peers[-1]
    mine = z * 2 + xh
    y_at = {1: y_peers[0], 2: y_peers[1], -2: y_peers[-2], -1: y_peers[-1]}
    z_at = {o: (r, (xh * 8 + (z + o + RING) % RING) * 2 + k) for o in (1, 2, -2, -1)}
    x_near = (y * 2 + 1 - xl, c)
    x_far = (r, ((1 - xh) * 8 + z) * 2 + k)
    other = (r, chip * 2 + 1 - k)
    x_other = (y * 2 + 1 - xl, chip * 2 + 1 - k)
    v_from = (chip, (xl * 8 + (y2 + z0) % 2 * 4 + (y1 + z1) % 2 * 2 + y0) * 2 + k)
    v_piece = (z2 + xl) % 2 * 4 + (z1 + y0) % 2 * 2 + z0
    v_to = (v_piece * 2 + xh, r * 2 + k)
    v_apart = jnp.logical_or(v_to[0] != r, v_to[1] != c)
    q = (z1 * 4 + z2 * 2 + z0) * 2 + xh
    z_to = (chip, (xl * 8 + y1 * 4 + y2 * 2 + y0) * 2 + k)
    z_from = (q, r * 2 + k)
    z_apart = jnp.logical_or(z_to[0] != r, z_to[1] != c)

    count = [0]
    started = []

    def copy(src, dst, device):
        slot = count[0]
        count[0] += 1
        return pltpu.make_async_remote_copy(
            src_ref=src, dst_ref=dst, send_sem=send_sems.at[slot], recv_sem=recv_sems.at[slot],
            device_id=device, device_id_type=pl.DeviceIdType.MESH)

    def go(op):
        op.start()
        started.append(op)
        return op

    barrier = pltpu.get_barrier_semaphore()

    def greet(device):
        pl.semaphore_signal(barrier, inc=1, device_id=device, device_id_type=pl.DeviceIdType.MESH)

    fixed = [*y_peers, x_near, x_other, *z_at.values(), x_far, other]
    for device in fixed:
        greet(device)

    @pl.when(v_apart)
    def _():
        greet(v_from)

    @pl.when(z_apart)
    def _():
        greet(z_from)

    loads = [pltpu.make_async_copy(src, dst, load_sems.at[i])
             for i, (src, dst) in enumerate(((v_hbm, v_ref), (a_hbm, a_ref), (t_hbm, t_ref)))]
    for load in loads:
        load.start()
    loads[0].wait()
    vh[...], vl[...] = split(v_ref[...])
    loads[1].wait()
    ah[...], al[...] = split(a_ref[...])

    def product(group):
        lanes = pl.ds(pl.multiple_of((group + 4) % 4 * 128, 128), 128)
        pt[lanes, :] = dot3((vh[:, lanes], vl[:, lanes]), (ah[...], al[...]), TN)

    far_group, side = (y + 4) // 2, 1 - 2 * ((y + 1) % 2)
    product(far_group)
    product(far_group + side)

    pl.semaphore_wait(barrier, len(fixed) + v_apart.astype(jnp.int32) + z_apart.astype(jnp.int32))

    def pt_at(part, index):
        return pl.ds(pl.multiple_of((index + RING) % RING * (2 * sub) + part * sub, sub), sub)

    NAMES = ("RA", "LB", "RB", "LA")
    first = {"RA": 0, "LB": 0, "RB": 1, "LA": 1}
    base = {"RA": 0, "LB": 4, "RB": 7, "LA": 10}
    rs = {}

    def rs_at(name, s):
        return pt_at(0 if name[1] == "A" else 1, y + 4 - s if name[0] == "R" else y - 4 + s)

    def rs_send(name, s):
        rs[name, s] = go(copy(pt.at[rs_at(name, s), :], rs_recv.at[base[name] + s], y_up if name[0] == "R" else y_down))

    def rs_round(s):
        for name in NAMES:
            if s - 1 >= first[name]:
                rs[name, s - 1].wait_recv()
                at = rs_at(name, s)
                pt[at, :] = pt[at, :] + rs_recv[base[name] + s - 1]
                rs_send(name, s)

    for name in NAMES:
        rs_send(name, first[name])

    v_rows = pl.ds(pl.multiple_of(v_piece * 2 * vsub, 8), 2 * vsub)
    v_src = pl.ds(pl.multiple_of(k * cols + v_piece * 2 * vsub, 8), 2 * vsub)
    v_copy = copy(v_ref.at[v_src, :], vcol.at[v_rows, :], v_to)

    @pl.when(v_apart)
    def _():
        v_copy.start()

    @pl.when(jnp.logical_not(v_apart))
    def _():
        vcol[v_rows, :] = v_ref[v_src, :]

    product(far_group - side)
    rs_round(1)
    product(far_group + 2)
    rs_round(2)

    half_rows = pl.ds(pl.multiple_of(k * cols, 128), cols)
    s21[...] = dot3((vh[half_rows, nb:], vl[half_rows, nb:]), (vh[half_rows, :nb], vl[half_rows, :nb]), TN)
    rs_round(3)

    def ring(half_of, me, up, down):
        ops = {}
        last = {"RA": 3, "LB": 3, "RB": 2, "LA": 2}

        def step(s, arrived=None):
            for name in NAMES:
                part = 0 if name[1] == "A" else 1
                index = (me - s + RING) % RING if name[0] == "R" else (me + s) % RING
                if s >= 1 and s - 1 <= last[name]:
                    ops[name, s - 1].wait_recv()
                if s <= last[name]:
                    ref = half_of(part, index)
                    ops[name, s] = go(copy(ref, ref, up if name[0] == "R" else down))
                if arrived is not None and s >= 1 and s - 1 <= last[name]:
                    arrived(part, index)

        return step

    def gather(whole, halves, me, at):
        ops = {}

        def near():
            for o in (1, -1, 2, -2):
                ops[o] = go(copy(whole(me), whole(me), at[o]))

        def on():
            for o in (2, -2):
                ops[o].wait_recv()
                index = (me - o + RING) % RING
                half_ref = halves(0 if o > 0 else 1, index)
                ops[o, 1] = go(copy(whole(index), whole(index), at[o // 2]))
                ops[o, 2] = go(copy(half_ref, half_ref, at[o]))
            for o in (1, -1):
                ops[o].wait_recv()

        def last():
            for o in (2, -2):
                ops[o, 1].wait_recv()
                ops[o, 2].wait_recv()

        return near, on, last

    def row_half(part, index):
        return zrow.at[k, pl.ds(pl.multiple_of(index * 2 * sub + part * sub, sub), sub), :]

    def g_chunk(index):
        return gfull.at[k, pl.ds(index * 2, 2)]

    def v_rows_of(start, size):
        return vcol.at[pl.ds(pl.multiple_of(start, 8), size), :]

    v_ring = ring(lambda h, i: v_rows_of(i * 2 * vsub + h * vsub, vsub), y, y_up, y_down)
    z_ring = ring(lambda h, i: zcol.at[pt_at(h, i), :], y, y_up, y_down)
    row_ring = ring(row_half, z, z_at[1], z_at[-1])
    g_gather = gather(g_chunk, lambda h, i: gfull.at[k, pl.ds(i * 2 + h, 1)], z, z_at)
    rows_over, g_over = [], []

    def pass_row(part, index):
        ref = row_half(part, index)
        rows_over.append(go(copy(ref, ref, other)))

    def pass_g(offsets):
        for o in offsets:
            ref = g_chunk((z + o + RING) % RING)
            g_over.append(go(copy(ref, ref, other)))

    @pl.when(v_apart)
    def _():
        v_copy.wait_recv()

    v_ring(0)
    for part, names in ((0, ("RA", "LA")), (1, ("LB", "RB"))):
        at = pt_at(part, y)
        total = pt[at, :]
        for name in names:
            rs[name, 3].wait_recv()
            total = total + rs_recv[base[name] + 3]
        pt[at, :] = total

    def zx_at(part):
        return pl.ds(pl.multiple_of(part * sub, sub), sub)

    x_ops = [go(copy(pt.at[pt_at(part, y), :], zx_recv.at[zx_at(part), :], x_near)) for part in (1 - xl, xl)]
    v_ring(1)

    own, rest = pt_at(xl, y), pt_at(1 - xl, y)
    x_ops[0].wait_recv()
    zcol[own, :] = pt[own, :] + zx_recv[zx_at(xl), :]
    z_rows = pl.ds(pl.multiple_of(((y1 * 4 + y2 * 2 + y0) * 2 + xl) * sub, sub), sub)
    z_copy = copy(zcol.at[own, :], zrow.at[k, z_rows, :], z_to)

    @pl.when(z_apart)
    def _():
        z_copy.start()

    @pl.when(jnp.logical_not(z_apart))
    def _():
        zrow[k, z_rows, :] = zcol[own, :]

    x_ops[1].wait_recv()
    zcol[rest, :] = pt[rest, :] + zx_recv[zx_at(1 - xl), :]
    z_ring(0)
    v_ring(2)

    @pl.when(z_apart)
    def _():
        z_copy.wait_recv()

    own_slot = pl.ds(pl.multiple_of(mine * sub, sub), sub)
    far_op = go(copy(zrow.at[k, own_slot, :], zrow.at[k, own_slot, :], x_far))
    part = dot3(split(zrow[k, own_slot, :]), (vh[half_rows, :], vl[half_rows, :]), NN)
    s_rows = s21[pl.ds(pl.multiple_of(q % 8 * sub, sub), sub), :]
    gloc[:, :nb] = jnp.where(q >= 8, s_rows, part[:, :nb])
    gloc[:, nb:] = part[:, nb:]
    my_half = pl.ds(pl.multiple_of(k * half, half), half)
    its_half = pl.ds(pl.multiple_of((1 - k) * half, half), half)
    ga = [go(copy(gloc.at[its_half, :], ga_recv.at[0], x_other)),
          go(copy(gloc.at[my_half, :], ga_recv.at[1], x_near)),
          go(copy(gloc.at[its_half, :], ga_recv.at[2], other))]
    far_op.wait_recv()
    row_ring(0)
    pass_row(xh, z)
    z_ring(1)
    total = gloc[my_half, :]
    for i in (2, 1, 0):
        ga[i].wait_recv()
        total = total + ga_recv[i]
    for j in range(8):
        gtiles[j] = total[j // 4 * 8:j // 4 * 8 + 8, j % 4 * 128:(j % 4 + 1) * 128]
    gc = [go(copy(gtiles.at[(y + o) % RING], gc_recv.at[o], y_peers[o - 1])) for o in range(1, RING)]
    pass_row(1 - xh, z)
    row_ring(1, pass_row)
    v_ring(3)
    tile = gtiles[y]
    for o in range(1, RING):
        gc[o - 1].wait_recv()
        tile = tile + gc_recv[o]
    gfull[k, mine, y] = tile
    gd = [go(copy(gfull.at[k, mine, y], gfull.at[k, mine, y], y_peers[o - 1])) for o in range(1, RING)]
    row_ring(2, pass_row)
    z_ring(2)
    v_ring(4)

    loads[2].wait()
    t1, t2 = split(t_ref[0]), split(t_ref[1])
    v1, v2 = split(vcol[:, :nb]), split(vcol[:, nb:])
    for p, (t, v) in enumerate(((t1, v1), (t2, v2))):
        u_high, u_low = split(dot3(t, v, NT))
        for i in range(8):
            at = SLOT[p * 8 + i] * sub
            uh[at:at + sub, :] = u_high[i * sub:(i + 1) * sub, :]
            ul[at:at + sub, :] = u_low[i * sub:(i + 1) * sub, :]
    for op in gd:
        op.wait_recv()
    ge = go(copy(gfull.at[k, mine], gfull.at[k, mine], x_far))
    row_ring(3, pass_row)
    z_ring(3)
    ge.wait_recv()
    g_gather[0]()
    pass_g((0,))
    row_ring(4, pass_row)
    z_ring(4)
    yt1 = dot3(t1, split(zcol[:nb, :]), TN)
    yt1_ref[...] = yt1
    qh[:nb, :], ql[:nb, :] = split(yt1)
    qh[nb:, :], ql[nb:, :] = split(dot3(t2, split(zcol[nb:, :]), TN))
    def tiles(i):
        for h in range(2):
            at = pl.ds(pl.multiple_of(h * cols + i * 128, 128), 128)
            yield h, at, pl.ds(pl.multiple_of(i * 128, 128), 128)

    def early(i, _):
        for h, at, lanes in tiles(i):
            acc = dot3((vh[at, :], vl[at, :]), (qh[...], ql[...]), NN)
            upd_ref[at, :] = -acc - dot3(split(zrow[h, :, lanes]), (uh[...], ul[...]), TN)
        return 0

    def late(i, _):
        for h, at, lanes in tiles(i):
            acc = dot3((vh[at, :], vl[at, :]), (qh[...], ql[...]), NN)
            kept = jnp.concatenate([zrow[h, s * sub:(s + 1) * sub, lanes] for s in FIRST], axis=0)
            upd_ref[at, :] = upd_ref[at, :] - acc - dot3(split(kept), (uh[:nb, :], ul[:nb, :]), TN)
        return 0

    g_gather[1]()
    pass_g((1, -1, 2, -2))
    for op in rows_over:
        op.wait_recv()
    lax.fori_loop(0, 3, early, 0)
    g_gather[2]()
    pass_g((3, -3, 4))
    for op in g_over:
        op.wait_recv()

    def block(row, col):
        lanes = []
        for j in (2 * col, 2 * col + 1):
            found = [gfull[core, SLOT[i], h * 4 + j]
                     for i in range(row * 8, row * 8 + 8) for core in range(2) for h in range(2)]
            lanes.append(jnp.concatenate(found, axis=0))
        return jnp.concatenate(lanes, axis=1)

    g11, g12, s_21, g22 = block(0, 0), block(0, 1), block(1, 0), block(1, 1)
    s_21s = split(s_21)
    s_12s = split(s_21.T)
    e = dot3(s_12s, t2, NN)
    es = split(e)
    m1 = dot3(t1, split(dot3(split(g11), t1, NN)), TN)
    m1s = split(m1)
    kk = dot3(t1, split(g12), TN) - 0.5 * dot3(m1s, s_12s, TN)
    kks = split(kk)
    jj = dot3(s_21s, kks, NN)
    m2 = dot3(t2, split(dot3(split(g22 - jj - jj.T), t2, NN)), TN)
    h12s = split(0.5 * dot3(m1s, es, NN) - dot3(kks, t2, NN))
    qh[:nb, :], ql[:nb, :] = split(dot3(h12s, v2, NT) - dot3(m1s, v1, NT))
    low_q = dot3(h12s, v1, (((0,), (1,)), ((), ()))) - dot3(split(m2), v2, NT)
    qh[nb:, :], ql[nb:, :] = split(low_q - dot3(es, split(yt1_ref[...]), TN))
    u_high, u_low = split(-dot3(t1, split(dot3(es, v2, NT)), NN))
    for at, s in enumerate(FIRST):
        i = SLOT.index(s)
        uh[at * sub:(at + 1) * sub, :] = u_high[i * sub:(i + 1) * sub, :]
        ul[at * sub:(at + 1) * sub, :] = u_low[i * sub:(i + 1) * sub, :]
    lax.fori_loop(0, cols // 128, late, 0)

    for op in started:
        op.wait_send()

    @pl.when(v_apart)
    def _():
        v_copy.wait_send()

    @pl.when(z_apart)
    def _():
        z_copy.wait_send()


COPIES = 14 + 2 + 2 + 14 + 14 + (1 + 14 + 16) + (3 + 7 + 7 + 1 + 8 + 8)


def body(matrix, reflectors, factors):
    rows, cols = matrix.shape
    width = reflectors.shape[1]
    nb = width // 2
    sub = width // 16
    vmem = pl.BlockSpec(memory_space=pltpu.VMEM)
    update = pl.pallas_call(
        kernel,
        out_shape=jax.ShapeDtypeStruct((rows, cols), F32),
        in_specs=[pl.BlockSpec(memory_space=pltpu.HBM)] * 3,
        out_specs=vmem,
        scratch_shapes=[
            pltpu.VMEM((rows, cols), F32),
            pltpu.VMEM((rows, width), F32),
            pltpu.VMEM(factors.shape, F32),
            pltpu.VMEM((rows, cols), BF16),
            pltpu.VMEM((rows, cols), BF16),
            pltpu.VMEM((rows, width), BF16),
            pltpu.VMEM((rows, width), BF16),
            pltpu.VMEM((width, cols), F32),
            pltpu.VMEM((14, sub, cols), F32),
            pltpu.VMEM((2 * sub, cols), F32),
            pltpu.VMEM((width, cols), F32),
            pltpu.VMEM((cols, width), F32),
            pltpu.VMEM((2, width, cols), F32),
            pltpu.VMEM((nb, nb), F32),
            pltpu.VMEM((sub, width), F32),
            pltpu.VMEM((3, sub // 2, width), F32),
            pltpu.VMEM((8, 8, 128), F32),
            pltpu.VMEM((8, 8, 128), F32),
            pltpu.VMEM((2, 16, 8, 8, 128), F32),
            pltpu.VMEM((width, cols), BF16),
            pltpu.VMEM((width, cols), BF16),
            pltpu.VMEM((width, cols), BF16),
            pltpu.VMEM((width, cols), BF16),
            pltpu.VMEM((nb, cols), F32),
            pltpu.SemaphoreType.DMA((3,)),
            pltpu.SemaphoreType.DMA((COPIES,)),
            pltpu.SemaphoreType.DMA((COPIES,)),
        ],
        compiler_params=pltpu.CompilerParams(
            collective_id=0, has_side_effects=True, vmem_limit_bytes=60 * 1024 * 1024),
        name="two_panels",
    )(matrix, reflectors, factors)
    return matrix + update


def solution(mesh):
    return jax.shard_map(
        body,
        mesh=mesh,
        in_specs=(P("prow", "pcol"), P("prow", None), P()),
        out_specs=P("prow", "pcol"),
        check_vma=False,
    )
```

```python
import jax
import jax.numpy as jnp
from jax import lax
from jax.experimental import pallas as pl
from jax.experimental.pallas import tpu as pltpu
from jax.sharding import PartitionSpec as P

F32 = jnp.float32
BF16 = jnp.bfloat16
RING = 8
NN = (((1,), (0,)), ((), ()))
TN = (((0,), (0,)), ((), ()))
NT = (((1,), (1,)), ((), ()))


def split(x):
    high = x.astype(BF16)
    return high, (x - high.astype(F32)).astype(BF16)


def dot3(left, right, dims):
    (lh, ll), (rh, rl) = left, right
    def one(p, q):
        return lax.dot_general(p, q, dims, preferred_element_type=F32)
    return one(lh, rh) + (one(lh, rl) + one(ll, rh))


def mm(left, right, dims):
    return dot3(split(left), split(right), dims)


def slot_of(q):
    y, xl = q // 2, q % 2
    return (y // 2 % 2 * 4 + y // 4 * 2 + y % 2) * 2 + xl


SLOT = [slot_of(q) for q in range(16)]
FIRST = sorted(SLOT[:8])


def kernel(a_hbm, v_hbm, t_hbm, upd_ref, a_ref, v_ref, t_ref, ah, al, vh, vl, pt, rs_recv, zx_recv, zcol, vcol,
           zrow, s21, gloc, ga_recv, gtiles, gc_recv, gfull, qh, ql, uh, ul, yt1_ref, load_sems, send_sems, recv_sems):
    width = v_ref.shape[1]
    cols = a_ref.shape[1]
    nb = width // 2
    sub = width // 16
    vsub = cols // 16
    half = sub // 2
    r = lax.axis_index("prow")
    c = lax.axis_index("pcol")
    y, xl = r // 2, r % 2
    chip, k = c // 2, c % 2
    xh, z = chip // 8, chip % 8
    y2, y1, y0 = y // 4, y // 2 % 2, y % 2
    z2, z1, z0 = z // 4, z // 2 % 2, z % 2

    y_peers = [((y + o) % RING * 2 + xl, c) for o in range(1, RING)]
    y_up, y_down = y_peers[0], y_peers[-1]
    mine = z * 2 + xh
    y_at = {1: y_peers[0], 2: y_peers[1], -2: y_peers[-2], -1: y_peers[-1]}
    z_at = {o: (r, (xh * 8 + (z + o + RING) % RING) * 2 + k) for o in (1, 2, -2, -1)}
    x_near = (y * 2 + 1 - xl, c)
    x_far = (r, ((1 - xh) * 8 + z) * 2 + k)
    other = (r, chip * 2 + 1 - k)
    x_other = (y * 2 + 1 - xl, chip * 2 + 1 - k)
    v_from = (chip, (xl * 8 + (y2 + z0) % 2 * 4 + (y1 + z1) % 2 * 2 + y0) * 2 + k)
    v_piece = (z2 + xl) % 2 * 4 + (z1 + y0) % 2 * 2 + z0
    v_to = (v_piece * 2 + xh, r * 2 + k)
    v_apart = jnp.logical_or(v_to[0] != r, v_to[1] != c)
    q = (z1 * 4 + z2 * 2 + z0) * 2 + xh
    z_to = (chip, (xl * 8 + y1 * 4 + y2 * 2 + y0) * 2 + k)
    z_from = (q, r * 2 + k)
    z_apart = jnp.logical_or(z_to[0] != r, z_to[1] != c)

    count = [0]
    started = []

    def copy(src, dst, device):
        slot = count[0]
        count[0] += 1
        return pltpu.make_async_remote_copy(
            src_ref=src, dst_ref=dst, send_sem=send_sems.at[slot], recv_sem=recv_sems.at[slot],
            device_id=device, device_id_type=pl.DeviceIdType.MESH)

    def go(op):
        op.start()
        started.append(op)
        return op

    barrier = pltpu.get_barrier_semaphore()

    def greet(device):
        pl.semaphore_signal(barrier, inc=1, device_id=device, device_id_type=pl.DeviceIdType.MESH)

    fixed = [*y_peers, x_near, x_other, *z_at.values(), x_far, other]
    for device in fixed:
        greet(device)

    @pl.when(v_apart)
    def _():
        greet(v_from)

    @pl.when(z_apart)
    def _():
        greet(z_from)

    loads = [pltpu.make_async_copy(src, dst, load_sems.at[i])
             for i, (src, dst) in enumerate(((v_hbm, v_ref), (a_hbm, a_ref), (t_hbm, t_ref)))]
    for load in loads:
        load.start()
    loads[0].wait()
    vh[...], vl[...] = split(v_ref[...])
    loads[1].wait()
    ah[...], al[...] = split(a_ref[...])

    def product(group):
        lanes = pl.ds(pl.multiple_of((group + 4) % 4 * 128, 128), 128)
        pt[lanes, :] = dot3((vh[:, lanes], vl[:, lanes]), (ah[...], al[...]), TN)

    far_group, side = (y + 4) // 2, 1 - 2 * ((y + 1) % 2)
    product(far_group)
    product(far_group + side)

    pl.semaphore_wait(barrier, len(fixed) + v_apart.astype(jnp.int32) + z_apart.astype(jnp.int32))

    def pt_at(part, index):
        return pl.ds(pl.multiple_of((index + RING) % RING * (2 * sub) + part * sub, sub), sub)

    NAMES = ("RA", "LB", "RB", "LA")
    first = {"RA": 0, "LB": 0, "RB": 1, "LA": 1}
    base = {"RA": 0, "LB": 4, "RB": 7, "LA": 10}
    rs = {}

    def rs_at(name, s):
        return pt_at(0 if name[1] == "A" else 1, y + 4 - s if name[0] == "R" else y - 4 + s)

    def rs_send(name, s):
        rs[name, s] = go(copy(pt.at[rs_at(name, s), :], rs_recv.at[base[name] + s], y_up if name[0] == "R" else y_down))

    def rs_round(s):
        for name in NAMES:
            if s - 1 >= first[name]:
                rs[name, s - 1].wait_recv()
                at = rs_at(name, s)
                pt[at, :] = pt[at, :] + rs_recv[base[name] + s - 1]
                rs_send(name, s)

    for name in NAMES:
        rs_send(name, first[name])

    v_rows = pl.ds(pl.multiple_of(v_piece * 2 * vsub, 8), 2 * vsub)
    v_src = pl.ds(pl.multiple_of(k * cols + v_piece * 2 * vsub, 8), 2 * vsub)
    v_copy = copy(v_ref.at[v_src, :], vcol.at[v_rows, :], v_to)

    product(far_group - side)
    rs_round(1)
    product(far_group + 2)
    rs_round(2)

    half_rows = pl.ds(pl.multiple_of(k * cols, 128), cols)
    s21[...] = dot3((vh[half_rows, nb:], vl[half_rows, nb:]), (vh[half_rows, :nb], vl[half_rows, :nb]), TN)
    rs_round(3)

    @pl.when(v_apart)
    def _():
        v_copy.start()

    @pl.when(jnp.logical_not(v_apart))
    def _():
        vcol[v_rows, :] = v_ref[v_src, :]

    def ring(half_of, me, up, down):
        ops = {}
        last = {"RA": 3, "LB": 3, "RB": 2, "LA": 2}

        def step(s, arrived=None):
            for name in NAMES:
                part = 0 if name[1] == "A" else 1
                index = (me - s + RING) % RING if name[0] == "R" else (me + s) % RING
                if s >= 1 and s - 1 <= last[name]:
                    ops[name, s - 1].wait_recv()
                if s <= last[name]:
                    ref = half_of(part, index)
                    ops[name, s] = go(copy(ref, ref, up if name[0] == "R" else down))
                if arrived is not None and s >= 1 and s - 1 <= last[name]:
                    arrived(part, index)

        return step

    def gather(whole, halves, me, at):
        ops = {}

        def near():
            for o in (1, -1, 2, -2):
                ops[o] = go(copy(whole(me), whole(me), at[o]))

        def on():
            for o in (2, -2):
                ops[o].wait_recv()
                index = (me - o + RING) % RING
                half_ref = halves(0 if o > 0 else 1, index)
                ops[o, 1] = go(copy(whole(index), whole(index), at[o // 2]))
                ops[o, 2] = go(copy(half_ref, half_ref, at[o]))
            for o in (1, -1):
                ops[o].wait_recv()

        def last():
            for o in (2, -2):
                ops[o, 1].wait_recv()
                ops[o, 2].wait_recv()

        return near, on, last

    def row_half(part, index):
        return zrow.at[k, pl.ds(pl.multiple_of(index * 2 * sub + part * sub, sub), sub), :]

    def g_chunk(index):
        return gfull.at[k, pl.ds(index * 2, 2)]

    def v_rows_of(start, size):
        return vcol.at[pl.ds(pl.multiple_of(start, 8), size), :]

    v_ring = ring(lambda h, i: v_rows_of(i * 2 * vsub + h * vsub, vsub), y, y_up, y_down)
    z_ring = ring(lambda h, i: zcol.at[pt_at(h, i), :], y, y_up, y_down)
    row_ring = ring(row_half, z, z_at[1], z_at[-1])
    g_gather = gather(g_chunk, lambda h, i: gfull.at[k, pl.ds(i * 2 + h, 1)], z, z_at)
    rows_over, g_over = [], []

    def pass_row(part, index):
        ref = row_half(part, index)
        rows_over.append(go(copy(ref, ref, other)))

    def pass_g(offsets):
        for o in offsets:
            ref = g_chunk((z + o + RING) % RING)
            g_over.append(go(copy(ref, ref, other)))

    for part, names in ((0, ("RA", "LA")), (1, ("LB", "RB"))):
        at = pt_at(part, y)
        total = pt[at, :]
        for name in names:
            rs[name, 3].wait_recv()
            total = total + rs_recv[base[name] + 3]
        pt[at, :] = total

    def zx_at(part):
        return pl.ds(pl.multiple_of(part * sub, sub), sub)

    x_ops = [go(copy(pt.at[pt_at(part, y), :], zx_recv.at[zx_at(part), :], x_near)) for part in (1 - xl, xl)]

    own, rest = pt_at(xl, y), pt_at(1 - xl, y)
    x_ops[0].wait_recv()
    zcol[own, :] = pt[own, :] + zx_recv[zx_at(xl), :]
    z_rows = pl.ds(pl.multiple_of(((y1 * 4 + y2 * 2 + y0) * 2 + xl) * sub, sub), sub)
    z_copy = copy(zcol.at[own, :], zrow.at[k, z_rows, :], z_to)

    @pl.when(z_apart)
    def _():
        z_copy.start()

    @pl.when(jnp.logical_not(z_apart))
    def _():
        zrow[k, z_rows, :] = zcol[own, :]

    x_ops[1].wait_recv()
    zcol[rest, :] = pt[rest, :] + zx_recv[zx_at(1 - xl), :]
    z_ring(0)

    @pl.when(v_apart)
    def _():
        v_copy.wait_recv()

    v_ring(0)

    @pl.when(z_apart)
    def _():
        z_copy.wait_recv()

    own_slot = pl.ds(pl.multiple_of(mine * sub, sub), sub)
    far_op = go(copy(zrow.at[k, own_slot, :], zrow.at[k, own_slot, :], x_far))
    part = dot3(split(zrow[k, own_slot, :]), (vh[half_rows, :], vl[half_rows, :]), NN)
    s_rows = s21[pl.ds(pl.multiple_of(q % 8 * sub, sub), sub), :]
    gloc[:, :nb] = jnp.where(q >= 8, s_rows, part[:, :nb])
    gloc[:, nb:] = part[:, nb:]
    my_half = pl.ds(pl.multiple_of(k * half, half), half)
    its_half = pl.ds(pl.multiple_of((1 - k) * half, half), half)
    ga = [go(copy(gloc.at[its_half, :], ga_recv.at[0], x_other)),
          go(copy(gloc.at[my_half, :], ga_recv.at[1], x_near)),
          go(copy(gloc.at[its_half, :], ga_recv.at[2], other))]
    far_op.wait_recv()
    row_ring(0)
    pass_row(xh, z)
    z_ring(1)
    v_ring(1)
    total = gloc[my_half, :]
    for i in (2, 1, 0):
        ga[i].wait_recv()
        total = total + ga_recv[i]
    for j in range(8):
        gtiles[j] = total[j // 4 * 8:j // 4 * 8 + 8, j % 4 * 128:(j % 4 + 1) * 128]
    gc = [go(copy(gtiles.at[(y + o) % RING], gc_recv.at[o], y_peers[o - 1])) for o in range(1, RING)]
    pass_row(1 - xh, z)
    row_ring(1, pass_row)
    v_ring(2)
    tile = gtiles[y]
    for o in range(1, RING):
        gc[o - 1].wait_recv()
        tile = tile + gc_recv[o]
    gfull[k, mine, y] = tile
    gd = [go(copy(gfull.at[k, mine, y], gfull.at[k, mine, y], y_peers[o - 1])) for o in range(1, RING)]
    row_ring(2, pass_row)
    z_ring(2)
    v_ring(3)

    for op in gd:
        op.wait_recv()
    ge = go(copy(gfull.at[k, mine], gfull.at[k, mine], x_far))
    row_ring(3, pass_row)
    z_ring(3)
    ge.wait_recv()
    g_gather[0]()
    pass_g((0,))
    row_ring(4, pass_row)
    z_ring(4)
    v_ring(4)

    loads[2].wait()
    t1, t2 = split(t_ref[0]), split(t_ref[1])
    v1, v2 = split(vcol[:, :nb]), split(vcol[:, nb:])
    for p, (t, v) in enumerate(((t1, v1), (t2, v2))):
        u_high, u_low = split(dot3(t, v, NT))
        for i in range(8):
            at = SLOT[p * 8 + i] * sub
            uh[at:at + sub, :] = u_high[i * sub:(i + 1) * sub, :]
            ul[at:at + sub, :] = u_low[i * sub:(i + 1) * sub, :]
    yt1 = dot3(t1, split(zcol[:nb, :]), TN)
    yt1_ref[...] = yt1
    qh[:nb, :], ql[:nb, :] = split(yt1)
    qh[nb:, :], ql[nb:, :] = split(dot3(t2, split(zcol[nb:, :]), TN))
    def tiles(i):
        for h in range(2):
            at = pl.ds(pl.multiple_of(h * cols + i * 128, 128), 128)
            yield h, at, pl.ds(pl.multiple_of(i * 128, 128), 128)

    def early(i, _):
        for h, at, lanes in tiles(i):
            acc = dot3((vh[at, :], vl[at, :]), (qh[...], ql[...]), NN)
            upd_ref[at, :] = -acc - dot3(split(zrow[h, :, lanes]), (uh[...], ul[...]), TN)
        return 0

    def late(i, _):
        for h, at, lanes in tiles(i):
            acc = dot3((vh[at, :], vl[at, :]), (qh[...], ql[...]), NN)
            kept = jnp.concatenate([zrow[h, s * sub:(s + 1) * sub, lanes] for s in FIRST], axis=0)
            upd_ref[at, :] = upd_ref[at, :] - acc - dot3(split(kept), (uh[:nb, :], ul[:nb, :]), TN)
        return 0

    g_gather[1]()
    pass_g((1, -1, 2, -2))
    for op in rows_over:
        op.wait_recv()
    lax.fori_loop(0, 3, early, 0)
    g_gather[2]()
    pass_g((3, -3, 4))
    for op in g_over:
        op.wait_recv()

    def block(row, col):
        lanes = []
        for j in (2 * col, 2 * col + 1):
            found = [gfull[core, SLOT[i], h * 4 + j]
                     for i in range(row * 8, row * 8 + 8) for core in range(2) for h in range(2)]
            lanes.append(jnp.concatenate(found, axis=0))
        return jnp.concatenate(lanes, axis=1)

    g11, g12, s_21, g22 = block(0, 0), block(0, 1), block(1, 0), block(1, 1)
    s_21s = split(s_21)
    s_12s = split(s_21.T)
    e = dot3(s_12s, t2, NN)
    es = split(e)
    m1 = dot3(t1, split(dot3(split(g11), t1, NN)), TN)
    m1s = split(m1)
    kk = dot3(t1, split(g12), TN) - 0.5 * dot3(m1s, s_12s, TN)
    kks = split(kk)
    jj = dot3(s_21s, kks, NN)
    m2 = dot3(t2, split(dot3(split(g22 - jj - jj.T), t2, NN)), TN)
    h12s = split(0.5 * dot3(m1s, es, NN) - dot3(kks, t2, NN))
    qh[:nb, :], ql[:nb, :] = split(dot3(h12s, v2, NT) - dot3(m1s, v1, NT))
    low_q = dot3(h12s, v1, (((0,), (1,)), ((), ()))) - dot3(split(m2), v2, NT)
    qh[nb:, :], ql[nb:, :] = split(low_q - dot3(es, split(yt1_ref[...]), TN))
    u_high, u_low = split(-dot3(t1, split(dot3(es, v2, NT)), NN))
    for at, s in enumerate(FIRST):
        i = SLOT.index(s)
        uh[at * sub:(at + 1) * sub, :] = u_high[i * sub:(i + 1) * sub, :]
        ul[at * sub:(at + 1) * sub, :] = u_low[i * sub:(i + 1) * sub, :]
    lax.fori_loop(0, cols // 128, late, 0)

    for op in started:
        op.wait_send()

    @pl.when(v_apart)
    def _():
        v_copy.wait_send()

    @pl.when(z_apart)
    def _():
        z_copy.wait_send()


COPIES = 14 + 2 + 2 + 14 + 14 + (1 + 14 + 16) + (3 + 7 + 7 + 1 + 8 + 8)


def body(matrix, reflectors, factors):
    rows, cols = matrix.shape
    width = reflectors.shape[1]
    nb = width // 2
    sub = width // 16
    vmem = pl.BlockSpec(memory_space=pltpu.VMEM)
    update = pl.pallas_call(
        kernel,
        out_shape=jax.ShapeDtypeStruct((rows, cols), F32),
        in_specs=[pl.BlockSpec(memory_space=pltpu.HBM)] * 3,
        out_specs=vmem,
        scratch_shapes=[
            pltpu.VMEM((rows, cols), F32),
            pltpu.VMEM((rows, width), F32),
            pltpu.VMEM(factors.shape, F32),
            pltpu.VMEM((rows, cols), BF16),
            pltpu.VMEM((rows, cols), BF16),
            pltpu.VMEM((rows, width), BF16),
            pltpu.VMEM((rows, width), BF16),
            pltpu.VMEM((width, cols), F32),
            pltpu.VMEM((14, sub, cols), F32),
            pltpu.VMEM((2 * sub, cols), F32),
            pltpu.VMEM((width, cols), F32),
            pltpu.VMEM((cols, width), F32),
            pltpu.VMEM((2, width, cols), F32),
            pltpu.VMEM((nb, nb), F32),
            pltpu.VMEM((sub, width), F32),
            pltpu.VMEM((3, sub // 2, width), F32),
            pltpu.VMEM((8, 8, 128), F32),
            pltpu.VMEM((8, 8, 128), F32),
            pltpu.VMEM((2, 16, 8, 8, 128), F32),
            pltpu.VMEM((width, cols), BF16),
            pltpu.VMEM((width, cols), BF16),
            pltpu.VMEM((width, cols), BF16),
            pltpu.VMEM((width, cols), BF16),
            pltpu.VMEM((nb, cols), F32),
            pltpu.SemaphoreType.DMA((3,)),
            pltpu.SemaphoreType.DMA((COPIES,)),
            pltpu.SemaphoreType.DMA((COPIES,)),
        ],
        compiler_params=pltpu.CompilerParams(
            collective_id=0, has_side_effects=True, vmem_limit_bytes=60 * 1024 * 1024),
        name="two_panels",
    )(matrix, reflectors, factors)
    return matrix + update


def solution(mesh):
    return jax.shard_map(
        body,
        mesh=mesh,
        in_specs=(P("prow", "pcol"), P("prow", None), P()),
        out_specs=P("prow", "pcol"),
        check_vma=False,
    )
```
